32 devices in a mesh: row: 4 (over y, x), col: 8 (over z, core).
Axes of the slice: x: 2, y: 2, z: 4, core: 2. Of those that a mesh axis runs over, the one named last changes fastest.
Arguments:
- amps: float32 [4096, 9216], P('row', 'col'), may hold values from -6 to 6
- ladder_ints: float32 [4096, 4096], P('row', 'col'), may hold values from -0.25 to 0.25
- cycle_ints: float32 [6144, 6144], P(None, 'row'), may hold values from -0.21875 to 0.21875
- virt_irrep: int32 [64], replicated, may hold values from 0 to 7
- occ_irrep: int32 [96], replicated, may hold values from 0 to 7
- virt_energy: float32 [64], replicated, may hold values from 0.5 to 3
- occ_energy: float32 [96], replicated, may hold values from -3 to -0.5
Outputs:
- update: float32 [4096, 9216], P('row', 'col')
The draws below stay inside these ranges and needn't reach their ends.
All inputs are finite; a program needn't handle non-finite values.
Results may differ from the reference program's by a relative error of at most 0.00005.
Values sent between devices are 32-bit elements; how exact they have to be, the bound alone decides.
No kernel may reach another device: no remote copies, remote signals or barrier semaphores. Data moves between devices by JAX's collectives and lax.ppermute only.
A program may use at most 192 MiB of HBM per device.

```python
import jax
import jax.numpy as jnp
from jax import lax

VS = 64
OS = 96
P_SIZE = 4096
IJ = 9216
Q = 6144


def with_ends(drawn, rng, low, high):
    dims = drawn.shape
    spot = [jax.random.randint(jax.random.fold_in(rng, axis), (), 0, dims[axis]) for axis in range(len(dims))]
    drawn = drawn.at[tuple(spot)].set(low)
    longest = dims.index(max(dims))
    spot[longest] = (spot[longest] + 1) % dims[longest]
    return drawn.at[tuple(spot)].set(high)


def steps_of(rng, dims, shards, least, top_value):
    gain = 1.0
    for dim, shards_of in shards:
        steps = jax.random.uniform(jax.random.fold_in(jax.random.fold_in(rng, 6), dim), (shards_of,), jnp.float32, least / len(shards), top_value / len(shards))
        gain = gain * jnp.repeat(jnp.exp(steps), dims[dim] // shards_of).reshape((-1,) + (1,) * (len(dims) - 1 - dim))
    return gain


def scatter_about(own_key, extent, deviation, reach, pieces=(), kind=jnp.bfloat16):
    drawn = jax.random.normal(own_key, extent, jnp.float32) * deviation
    if len(pieces) > 0:
        drawn = steps_of(own_key, extent, pieces, -0.22, 0.18) * drawn
    return jnp.clip(drawn, min=-reach, max=reach).astype(kind)


def setup_inputs(seed: int = 0) -> dict:
    streams_of = jax.random.split(jax.random.key(seed), 8)
    amps = scatter_about(streams_of[0], (P_SIZE, IJ), 1.0, 6.0, ((0, 4), (1, 8)), jnp.float32)
    ladder_ints = scatter_about(streams_of[1], (P_SIZE, P_SIZE), (VS * VS // 8) ** -0.5, 0.25, ((0, 4), (1, 8)), jnp.float32)
    cycle_ints = scatter_about(streams_of[2], (Q, Q), (VS * OS // 8) ** -0.5, 0.21875, ((1, 4),), jnp.float32)
    virt_irrep = with_ends(jax.random.randint(streams_of[3], (VS,), 0, 8), jax.random.fold_in(streams_of[3], 1), 0, 7).astype(jnp.int32)
    occ_irrep = with_ends(jax.random.randint(streams_of[4], (OS,), 0, 8), jax.random.fold_in(streams_of[4], 1), 0, 7).astype(jnp.int32)
    virt_energy = jnp.clip(jax.random.uniform(streams_of[5], (VS,), jnp.float32, 0.5, 3.0), 0.5, 3.0)
    occ_energy = jnp.clip(jax.random.uniform(streams_of[6], (OS,), jnp.float32, -3.0, -0.5), -3.0, -0.5)
    return dict(amps=amps, ladder_ints=ladder_ints, cycle_ints=cycle_ints, virt_irrep=virt_irrep, occ_irrep=occ_irrep, virt_energy=virt_energy, occ_energy=occ_energy)


def pair_labels(first, second):
    return jnp.bitwise_xor(first[:, None], second[None, :]).reshape(-1)


def reference(amps, ladder_ints, cycle_ints, virt_irrep, occ_irrep, virt_energy, occ_energy):
    highest = lax.Precision.HIGHEST
    virt_pairs = pair_labels(virt_irrep, virt_irrep)
    ladder_masked = jnp.where(virt_pairs[:, None] == virt_pairs[None, :], ladder_ints, jnp.float32(0.0))
    ladder = jnp.dot(ladder_masked, amps, precision=highest, preferred_element_type=jnp.float32)
    cycle_amps = amps.reshape(VS, VS, OS, OS).transpose(0, 2, 1, 3).reshape(VS * OS, VS * OS)
    mixed_pairs = pair_labels(virt_irrep, occ_irrep)
    cycle_masked = jnp.where(mixed_pairs[:, None] == mixed_pairs[None, :], cycle_ints, jnp.float32(0.0))
    cycle = jnp.dot(cycle_masked, cycle_amps, precision=highest, preferred_element_type=jnp.float32)
    cycle_back = cycle.reshape(VS, OS, VS, OS).transpose(0, 2, 1, 3).reshape(VS * VS, OS * OS)
    row_energy = (virt_energy[:, None] + virt_energy[None, :]).reshape(-1)
    col_energy = (occ_energy[:, None] + occ_energy[None, :]).reshape(-1)
    return (ladder + cycle_back) / (row_energy[:, None] - col_energy[None, :])
```

```python
import functools

import jax
import jax.numpy as jnp
from jax import lax
from jax.experimental import pallas as pl
from jax.experimental.pallas import tpu as pltpu
from jax.sharding import PartitionSpec as P

PARTS = 4
WINDOW = 128
TILE = 256
SMALL = pl.CostEstimate(flops=0, bytes_accessed=0, transcendentals=0)
PARAMS = pltpu.CompilerParams(vmem_limit_bytes=56 * 1024 * 1024)


def pair_labels(first, second):
    return jnp.bitwise_xor(first[:, None], second[None, :]).reshape(-1)


def halves(value):
    high = value.astype(jnp.bfloat16)
    return high, (value - high.astype(jnp.float32)).astype(jnp.bfloat16)


def dot(left, right):
    return jnp.dot(left, right, preferred_element_type=jnp.float32)


def to_cycle_kernel(occ, depth, moved_ref, high_ref, low_ref, cells, rows):
    _, height, width = moved_ref.shape
    sources, count = height // depth, width // occ
    for source in range(sources):
        value = moved_ref[0, source * depth : (source + 1) * depth, :]
        for k in range(count):
            at = (source * count + k) * 8
            cells[at : at + depth, 0:occ] = value[:, k * occ : (k + 1) * occ]
    for d in range(depth):
        value = cells[pl.ds(d, sources * count, stride=8), :]
        rows[:, d * occ : (d + 1) * occ] = value[:, 0:occ]
    high, low = halves(rows[...])
    high_ref[...] = high
    low_ref[...] = low


def to_cycle_rows(moved, occ):
    count, sources, depth, width = moved.shape
    height = sources * width // occ
    shape = jax.ShapeDtypeStruct((count * height, depth * occ), jnp.bfloat16)
    return pl.pallas_call(
        functools.partial(to_cycle_kernel, occ, depth),
        grid=(count,),
        in_specs=[pl.BlockSpec((1, sources * depth, width), lambda c: (c, 0, 0))],
        out_specs=[pl.BlockSpec((height, depth * occ), lambda c: (c, 0))] * 2,
        out_shape=[shape, shape],
        scratch_shapes=[
            pltpu.VMEM((height * 8, 128), jnp.float32),
            pltpu.VMEM((height, depth * occ), jnp.float32),
        ],
        compiler_params=PARAMS,
        cost_estimate=SMALL,
        name="to_cycle_rows",
    )(moved.reshape(count, sources * depth, width))


def cycle_kernel(
    base, ints_ref, rows_ref, own_ref, high_0, low_0, high_1, low_1, send_y, send_x, keep_y, keep_x
):
    step = pl.program_id(0)
    masked = jnp.where(rows_ref[...] == own_ref[...], ints_ref[...], jnp.float32(0.0))
    high, low = halves(masked)
    middle = high_0.shape[0]
    total = dot(low[:, :middle], high_0[...]) + dot(low[:, middle:], high_1[...])
    total += dot(high[:, :middle], low_0[...]) + dot(high[:, middle:], low_1[...])
    total += dot(high[:, :middle], high_0[...]) + dot(high[:, middle:], high_1[...])
    half = total.shape[0] // 2

    @pl.when(step < 2)
    def _():
        send_y[0] = total[:half]

    @pl.when(step >= 2)
    def _():
        keep_y[0] = total[:half]

    @pl.when(step % 2 == 0)
    def _():
        send_x[0] = total[half:]

    @pl.when(step % 2 == 1)
    def _():
        keep_x[0] = total[half:]


def cycle_sums(part, row_index, ints, labels, own_labels, rights):
    depth = ints.shape[1]
    width = rights[0].shape[1]
    height = ints.shape[0] // 4 // PARTS
    base = jnp.reshape(row_index, (1,)).astype(jnp.int32)

    def at(step, base):
        return (base[0] ^ (3 - step)) * PARTS + part, 0

    def still(step, base):
        return 0, 0

    shape = jax.ShapeDtypeStruct((2, height // 2, width), jnp.float32)
    block = (1, height // 2, width)
    return pl.pallas_call(
        cycle_kernel,
        grid_spec=pltpu.PrefetchScalarGridSpec(
            num_scalar_prefetch=1,
            grid=(4,),
            in_specs=[
                pl.BlockSpec((height, depth), at),
                pl.BlockSpec((height, 1), at),
                pl.BlockSpec((1, depth), still),
            ]
            + [pl.BlockSpec(value.shape, still) for value in rights],
            out_specs=[
                pl.BlockSpec(block, lambda step, base: (jnp.where(step == 0, 1, 0), 0, 0)),
                pl.BlockSpec(block, lambda step, base: (jnp.where(step < 2, 1, 0), 0, 0)),
                pl.BlockSpec(block, lambda step, base: (jnp.where(step < 3, 1, 0), 0, 0)),
                pl.BlockSpec(block, lambda step, base: (jnp.where(step < 2, 1, 0), 0, 0)),
            ],
        ),
        out_shape=[shape] * 4,
        compiler_params=PARAMS,
        cost_estimate=SMALL,
        name="cycle_sums",
    )(base, ints, labels, own_labels, *rights)


def owner_kernel(occ_local, *refs):
    *values, out_ref = refs
    count, rows, _ = out_ref.shape
    virt = rows // occ_local
    for half in range(2):
        keep, near, far = values[half * 3 : half * 3 + 3]
        total = keep[0] + near[0] + far[0]
        for a in range(virt // 2):
            for target in range(count):
                begin = (a * count + target) * occ_local
                at = (half * virt // 2 + a) * occ_local
                out_ref[target, at : at + occ_local, :] = total[begin : begin + occ_local, :]


def owner_blocks(low, high, count, occ_local):
    _, height, width = low[0].shape
    rows = 2 * height // count
    return pl.pallas_call(
        functools.partial(owner_kernel, occ_local),
        grid=(1,),
        in_specs=[pl.BlockSpec((1, height, width), lambda step: (0, 0, 0))] * 6,
        out_specs=pl.BlockSpec((count, rows, width), lambda step: (0, 0, 0)),
        out_shape=jax.ShapeDtypeStruct((count, rows, width), jnp.float32),
        compiler_params=PARAMS,
        cost_estimate=SMALL,
        name="owner_blocks",
    )(*low, *high)


def update_kernel(occ, occ_local, at, back_ref, ladder_ref, rows_ref, cols_ref, out_ref, cells, rows):
    sources, height, width = back_ref.shape
    count = width // occ
    pad = -(-occ_local // 8) * 8
    for a in range(height // occ_local):
        for source in range(sources):
            value = back_ref[source, a * occ_local : (a + 1) * occ_local, :]
            for b in range(count):
                at = ((a * sources + source) * count + b) * pad
                cells[at : at + occ_local, 0:occ] = value[:, b * occ : (b + 1) * occ]
    for i in range(occ_local):
        value = cells[pl.ds(i, rows.shape[0], stride=pad), :]
        rows[:, i * occ : (i + 1) * occ] = value[:, 0:occ]
    out_ref[...] = (ladder_ref[...] + rows[...]) / (rows_ref[...] - cols_ref[...])


def with_cycle(part, back, ladder, row_energy, col_energy, occ, occ_local):
    sources, rows, width = back.shape
    columns = ladder.shape[1]
    height = rows // occ_local * sources * width // occ
    pad = -(-occ_local // 8) * 8
    block = pl.BlockSpec((height, columns), lambda step, at: (at[0], 0))
    return pl.pallas_call(
        functools.partial(update_kernel, occ, occ_local),
        grid_spec=pltpu.PrefetchScalarGridSpec(
            num_scalar_prefetch=1,
            grid=(1,),
            in_specs=[
                pl.BlockSpec(back.shape, lambda step, at: (0, 0, 0)),
                block,
                pl.BlockSpec((height, 1), lambda step, at: (0, 0)),
                pl.BlockSpec((1, columns), lambda step, at: (0, 0)),
            ],
            out_specs=block,
            scratch_shapes=[
                pltpu.VMEM((height * pad, 128), jnp.float32),
                pltpu.VMEM((height, columns), jnp.float32),
            ],
        ),
        out_shape=jax.ShapeDtypeStruct(ladder.shape, jnp.float32),
        input_output_aliases={2: 0},
        compiler_params=PARAMS,
        cost_estimate=SMALL,
        name="with_cycle",
    )(
        jnp.full((1,), part, jnp.int32),
        back,
        ladder,
        row_energy[part * height : (part + 1) * height],
        col_energy,
    )


def ladder_kernel(fresh, start, packed_ref, rank_ref, label_ref, own_ref, amps_ref, *refs):
    total_ref, (out_ref, high_ref, low_ref) = (None, refs) if fresh else (refs[0], refs[1:])

    @pl.when(pl.program_id(0) == 0)
    def _():
        high, low = halves(amps_ref[...])
        high_ref[...] = high
        low_ref[...] = low

    size, tile, window = packed_ref.shape
    wide = rank_ref.shape[2]
    total = None if fresh else total_ref[...]
    for n in range(size):
        pick = lax.broadcasted_iota(jnp.int32, (window, wide), 0) == rank_ref[n]
        pick = pick.astype(jnp.float32).astype(jnp.bfloat16)
        high, low = halves(packed_ref[n])
        ints = dot(high, pick) + dot(low, pick)
        ints = jnp.where(own_ref[...] == label_ref[n], ints, jnp.float32(0.0))
        high, low = halves(ints)
        at = slice(n * wide, (n + 1) * wide)
        term = dot(low, high_ref[at, :]) + dot(high, low_ref[at, :]) + dot(high, high_ref[at, :])
        total = term if total is None else total + term
    out_ref[...] = total


def ladder_term(start, packed, ranks, labels, own_pairs, amps, total=None):
    blocks, rows, window = packed.shape
    wide = ranks.shape[2]
    depth, columns = amps.shape
    size = depth // wide
    fresh = total is None
    out_block = pl.BlockSpec((TILE, columns), lambda m, start: (m, 0))
    small = pl.BlockSpec((size, 1, wide), lambda m, start: (start[0], 0, 0))
    return pl.pallas_call(
        functools.partial(ladder_kernel, fresh),
        grid_spec=pltpu.PrefetchScalarGridSpec(
            num_scalar_prefetch=1,
            grid=(rows // TILE,),
            in_specs=[
                pl.BlockSpec((size, TILE, window), lambda m, start: (start[0], m, 0)),
                small,
                small,
                pl.BlockSpec((TILE, 1), lambda m, start: (m, 0)),
                pl.BlockSpec((depth, columns), lambda m, start: (0, 0)),
            ]
            + ([] if fresh else [out_block]),
            out_specs=out_block,
            scratch_shapes=[pltpu.VMEM((depth, columns), jnp.bfloat16)] * 2,
        ),
        out_shape=jax.ShapeDtypeStruct((rows, columns), jnp.float32),
        input_output_aliases={} if fresh else {6: 0},
        compiler_params=PARAMS,
        cost_estimate=SMALL,
        name="ladder_term",
    )(
        jnp.reshape(start // size, (1,)).astype(jnp.int32),
        packed,
        ranks,
        labels,
        own_pairs,
        amps,
        *([] if fresh else [total]),
    )


def body(amps, ladder_ints, cycle_ints, virt_irrep, occ_irrep, virt_energy, occ_energy):
    row_count = lax.axis_size("row")
    col_count = lax.axis_size("col")
    row_index = lax.axis_index("row")
    col_index = lax.axis_index("col")
    virt_total = virt_irrep.shape[0]
    occ_total = occ_irrep.shape[0]
    virt_local = virt_total // row_count
    occ_local = occ_total // col_count
    virt_cols = virt_total // col_count
    pair_rows, columns = amps.shape
    ladder_cols = ladder_ints.shape[1]
    virt_pairs = pair_labels(virt_irrep, virt_irrep)
    own_pairs = lax.dynamic_slice_in_dim(virt_pairs, row_index * pair_rows, pair_rows)
    mixed_pairs = pair_labels(virt_irrep, occ_irrep)
    cycle_rows = virt_local * occ_total
    own_mixed = lax.dynamic_slice_in_dim(mixed_pairs, row_index * cycle_rows, cycle_rows)
    barrier = lax.optimization_barrier

    def swap(value, flip):
        return lax.ppermute(value, "row", [(i, i ^ flip) for i in range(row_count)])

    half_virt = virt_local // 2
    half_rows = pair_rows // 2
    first, second = amps[:half_rows], amps[half_rows:]

    def to_cycle(value):
        blocks = value.reshape(half_virt, col_count, virt_cols, columns)
        return lax.all_to_all(blocks, "col", split_axis=1, concat_axis=1, tiled=True)

    first_2, second_1 = swap(first, 2), swap(second, 1)
    moved = to_cycle(first)
    held_first, held, first_2, second_1, moved = barrier((first, second, first_2, second_1, moved))
    first_1, second_2 = swap(held_first, 1), swap(held, 2)
    rights = to_cycle_rows(moved, occ_total)
    moved = to_cycle(held)
    moved, first_1, second_2, first_2, second_1 = barrier(
        (moved, first_1, second_2, first_2, second_1)
    )
    first_3, second_3 = swap(first_2, 1), swap(second_1, 2)
    rights = rights + to_cycle_rows(moved, occ_total)

    blocks = virt_pairs.reshape(col_count, ladder_cols)
    place = jnp.arange(ladder_cols)
    same = (blocks[:, :, None] == blocks[:, None, :]) & (place[None, None, :] < place[None, :, None])
    rank = jnp.sum(same, axis=2, dtype=jnp.int32)
    turns = jnp.max(rank) // WINDOW + 1
    own_rank = lax.dynamic_index_in_dim(rank, col_index, 0, keepdims=False)
    own_block = lax.dynamic_index_in_dim(blocks, col_index, 0, keepdims=False)
    masked_ints = jnp.where(own_pairs[:, None] == own_block[None, :], ladder_ints, jnp.float32(0.0))

    def packed_ints(turn):
        pick = own_rank[:, None] == turn * WINDOW + jnp.arange(WINDOW)[None, :]
        return jnp.dot(
            masked_ints,
            pick.astype(jnp.float32),
            precision=lax.Precision.HIGH,
            preferred_element_type=jnp.float32,
        )

    def gathered(packed):
        return lax.all_gather(packed, "col", axis=0, tiled=False)

    def ladder_from(packed, turn, pieces, total=None):
        for flip, half, value in pieces:
            start = (row_index ^ flip) * (pair_rows // ladder_cols)
            start += half * (half_rows // ladder_cols)
            total = ladder_term(
                start,
                packed,
                rank[:, None, :] - turn * WINDOW,
                blocks[:, None, :],
                own_pairs[:, None],
                value,
                total,
            )
        return total

    packed, rights = barrier((packed_ints(0), rights))
    packed = gathered(packed)

    own_virt = lax.dynamic_slice_in_dim(virt_energy, row_index * virt_local, virt_local)
    own_occ = lax.dynamic_slice_in_dim(occ_energy, col_index * occ_local, occ_local)
    row_energy = (own_virt[:, None] + virt_energy[None, :]).reshape(-1)[:, None]
    col_energy = (own_occ[:, None] + occ_energy[None, :]).reshape(-1)[None, :]

    sums = functools.partial(
        cycle_sums, row_index=row_index, ints=cycle_ints, labels=mixed_pairs[:, None],
        own_labels=own_mixed[None, :],
    )
    def pass_on(keep, near):
        return swap(keep[0][1:] + near[0][1:], 1), swap(keep[1][1:] + near[1][1:], 2)

    def send(values):
        return swap(values[0], 2), swap(values[1], 1)

    def owned(keep, near, far):
        return owner_blocks(
            (keep[0], near[0], far[0]), (keep[1], near[1], far[1]), col_count, occ_local
        )

    def to_owner(blocks):
        return lax.all_to_all(blocks, "col", split_axis=0, concat_axis=0, tiled=True)

    def part_sums(part, rights):
        values = sums(part, rights=rights)
        return values[:2], values[2:]

    pieces = [(0, 0, first), (0, 1, second), (2, 0, first_2), (1, 1, second_1)]
    pieces += [(1, 0, first_1), (2, 1, second_2)]
    out_0, keep_0 = part_sums(0, rights)
    near_0 = send(out_0)
    rights, keep_0 = barrier((rights, keep_0))
    out_1, keep_1 = part_sums(1, rights)

    rights, first_3, second_3, near_0, keep_0, out_1, keep_1 = barrier(
        (rights, first_3, second_3, near_0, keep_0, out_1, keep_1)
    )
    pieces += [(3, 0, first_3), (3, 1, second_3)]
    far_0, near_1 = pass_on(keep_0, near_0), send(out_1)
    out_2, keep_2 = part_sums(2, rights)
    packed, keep_2 = barrier((packed, keep_2))
    ladder = ladder_from(packed, 0, pieces[:2])

    rights, ladder, far_0, near_0, keep_0, near_1, keep_1, out_2, keep_2 = barrier(
        (rights, ladder, far_0, near_0, keep_0, near_1, keep_1, out_2, keep_2)
    )
    far_1, near_2 = pass_on(keep_1, near_1), send(out_2)
    back_0 = to_owner(owned(keep_0, near_0, far_0))
    out_3, keep_3 = part_sums(3, rights)
    ladder, keep_3 = barrier((ladder, keep_3))
    ladder = ladder_from(packed, 0, pieces[2:4], ladder)

    ladder, back_0, far_1, near_1, keep_1, near_2, keep_2, out_3, keep_3 = barrier(
        (ladder, back_0, far_1, near_1, keep_1, near_2, keep_2, out_3, keep_3)
    )
    far_2, near_3 = pass_on(keep_2, near_2), send(out_3)
    back_1 = to_owner(owned(keep_1, near_1, far_1))
    ladder = ladder_from(packed, 0, pieces[4:7], ladder)

    ladder, back_1, far_2, near_2, keep_2, near_3, keep_3 = barrier(
        (ladder, back_1, far_2, near_2, keep_2, near_3, keep_3)
    )
    far_3 = pass_on(keep_3, near_3)
    back_2 = to_owner(owned(keep_2, near_2, far_2))
    ladder = ladder_from(packed, 0, pieces[7:], ladder)

    ladder, back_2, far_3, near_3, keep_3 = barrier((ladder, back_2, far_3, near_3, keep_3))
    back_3 = to_owner(owned(keep_3, near_3, far_3))
    backs = [back_0, back_1, back_2, back_3]
    update = ladder
    for part in range(PARTS):
        update = with_cycle(
            part, backs[part], update, row_energy, col_energy, occ_total, occ_local
        )
    return lax.fori_loop(
        1,
        turns,
        lambda turn, total: total
        + ladder_from(gathered(packed_ints(turn)), turn, pieces) / (row_energy - col_energy),
        update,
    )


def plain_body(
    amps, ladder_ints, cycle_ints, virt_irrep, occ_irrep, virt_energy, occ_energy
):
    high = lax.Precision.HIGH
    row_count = lax.axis_size("row")
    col_count = lax.axis_size("col")
    row_index = lax.axis_index("row")
    col_index = lax.axis_index("col")
    virt_total = virt_irrep.shape[0]
    occ_total = occ_irrep.shape[0]
    virt_local = virt_total // row_count
    occ_local = occ_total // col_count
    virt_cols = virt_total // col_count
    pair_rows = amps.shape[0]
    virt_pairs = pair_labels(virt_irrep, virt_irrep)
    own_pairs = lax.dynamic_slice_in_dim(virt_pairs, row_index * pair_rows, pair_rows)
    rows_full = lax.all_gather(ladder_ints, "col", axis=1, tiled=True)
    masked = jnp.where(own_pairs[:, None] == virt_pairs[None, :], rows_full, jnp.float32(0.0))
    ladder = jnp.dot(
        masked,
        lax.all_gather(amps, "row", axis=0, tiled=True),
        precision=high,
        preferred_element_type=jnp.float32,
    )
    blocks = amps.reshape(virt_local, virt_total, occ_local, occ_total)
    moved = lax.all_to_all(blocks, "col", split_axis=1, concat_axis=2, tiled=True)
    cycle_amps = moved.transpose(0, 2, 1, 3).reshape(virt_local * occ_total, virt_cols * occ_total)
    mixed_pairs = pair_labels(virt_irrep, occ_irrep)
    cycle_rows = cycle_amps.shape[0]
    own_mixed = lax.dynamic_slice_in_dim(mixed_pairs, row_index * cycle_rows, cycle_rows)
    part = cycle_ints
    part = jnp.where(mixed_pairs[:, None] == own_mixed[None, :], part, jnp.float32(0.0))
    cycle = lax.psum_scatter(
        jnp.dot(part, cycle_amps, precision=high, preferred_element_type=jnp.float32),
        "row",
        scatter_dimension=0,
        tiled=True,
    )
    cycle_blocks = cycle.reshape(virt_local, occ_total, virt_cols, occ_total)
    returned = lax.all_to_all(cycle_blocks, "col", split_axis=1, concat_axis=2, tiled=True)
    cycle_back = returned.transpose(0, 2, 1, 3).reshape(
        virt_local * virt_total, occ_local * occ_total
    )
    own_virt = lax.dynamic_slice_in_dim(virt_energy, row_index * virt_local, virt_local)
    own_occ = lax.dynamic_slice_in_dim(occ_energy, col_index * occ_local, occ_local)
    row_energy = (own_virt[:, None] + virt_energy[None, :]).reshape(-1)
    col_energy = (own_occ[:, None] + occ_energy[None, :]).reshape(-1)
    return (ladder + cycle_back) / (row_energy[:, None] - col_energy[None, :])


def solution(mesh):
    placed = (P("row", "col"), P("row", "col"), P(None, "row"), P(), P(), P(), P())
    plan = body if mesh.shape["row"] == 4 else plain_body
    return jax.shard_map(
        plan, mesh=mesh, in_specs=placed, out_specs=P("row", "col"), check_vma=False
    )
```

```python
import functools

import jax
import jax.numpy as jnp
from jax import lax
from jax.experimental import pallas as pl
from jax.experimental.pallas import tpu as pltpu
from jax.sharding import PartitionSpec as P

PARTS = 4
WINDOW = 128
TILE = 256
SMALL = pl.CostEstimate(flops=0, bytes_accessed=0, transcendentals=0)
PARAMS = pltpu.CompilerParams(vmem_limit_bytes=56 * 1024 * 1024)


def pair_labels(first, second):
    return jnp.bitwise_xor(first[:, None], second[None, :]).reshape(-1)


def halves(value):
    high = value.astype(jnp.bfloat16)
    return high, (value - high.astype(jnp.float32)).astype(jnp.bfloat16)


def dot(left, right):
    return jnp.dot(left, right, preferred_element_type=jnp.float32)


def to_cycle_kernel(occ, moved_ref, high_ref, low_ref, cells, rows):
    sources, _, depth, width = moved_ref.shape
    count = width // occ
    for source in range(sources):
        value = moved_ref[source, 0]
        for k in range(count):
            at = (source * count + k) * 8
            cells[at : at + depth, 0:occ] = value[:, k * occ : (k + 1) * occ]
    for d in range(depth):
        value = cells[pl.ds(d, sources * count, stride=8), :]
        rows[:, d * occ : (d + 1) * occ] = value[:, 0:occ]
    high, low = halves(rows[...])
    high_ref[...] = high
    low_ref[...] = low


def to_cycle_rows(moved, occ):
    sources, count, depth, width = moved.shape
    height = sources * width // occ
    shape = jax.ShapeDtypeStruct((count * height, depth * occ), jnp.bfloat16)
    return pl.pallas_call(
        functools.partial(to_cycle_kernel, occ),
        grid=(count,),
        in_specs=[pl.BlockSpec((sources, 1, depth, width), lambda c: (0, c, 0, 0))],
        out_specs=[pl.BlockSpec((height, depth * occ), lambda c: (c, 0))] * 2,
        out_shape=[shape, shape],
        scratch_shapes=[
            pltpu.VMEM((height * 8, 128), jnp.float32),
            pltpu.VMEM((height, depth * occ), jnp.float32),
        ],
        compiler_params=PARAMS,
        cost_estimate=SMALL,
        name="to_cycle_rows",
    )(moved)


def cycle_kernel(
    base, ints_ref, rows_ref, own_ref, high_0, low_0, high_1, low_1, send_y, send_x, keep_y, keep_x
):
    step = pl.program_id(0)
    masked = jnp.where(rows_ref[...] == own_ref[...], ints_ref[...], jnp.float32(0.0))
    high, low = halves(masked)
    middle = high_0.shape[0]
    total = dot(low[:, :middle], high_0[...]) + dot(low[:, middle:], high_1[...])
    total += dot(high[:, :middle], low_0[...]) + dot(high[:, middle:], low_1[...])
    total += dot(high[:, :middle], high_0[...]) + dot(high[:, middle:], high_1[...])
    half = total.shape[0] // 2

    @pl.when(step < 2)
    def _():
        send_y[0] = total[:half]

    @pl.when(step >= 2)
    def _():
        keep_y[0] = total[:half]

    @pl.when(step % 2 == 0)
    def _():
        send_x[0] = total[half:]

    @pl.when(step % 2 == 1)
    def _():
        keep_x[0] = total[half:]


def cycle_sums(part, row_index, ints, labels, own_labels, rights):
    depth = ints.shape[1]
    width = rights[0].shape[1]
    height = ints.shape[0] // 4 // PARTS
    base = jnp.reshape(row_index, (1,)).astype(jnp.int32)

    def at(step, base):
        return (base[0] ^ (3 - step)) * PARTS + part, 0

    def still(step, base):
        return 0, 0

    shape = jax.ShapeDtypeStruct((2, height // 2, width), jnp.float32)
    block = (1, height // 2, width)
    return pl.pallas_call(
        cycle_kernel,
        grid_spec=pltpu.PrefetchScalarGridSpec(
            num_scalar_prefetch=1,
            grid=(4,),
            in_specs=[
                pl.BlockSpec((height, depth), at),
                pl.BlockSpec((height, 1), at),
                pl.BlockSpec((1, depth), still),
            ]
            + [pl.BlockSpec(value.shape, still) for value in rights],
            out_specs=[
                pl.BlockSpec(block, lambda step, base: (jnp.where(step == 0, 1, 0), 0, 0)),
                pl.BlockSpec(block, lambda step, base: (jnp.where(step < 2, 1, 0), 0, 0)),
                pl.BlockSpec(block, lambda step, base: (jnp.where(step < 3, 1, 0), 0, 0)),
                pl.BlockSpec(block, lambda step, base: (jnp.where(step < 2, 1, 0), 0, 0)),
            ],
        ),
        out_shape=[shape] * 4,
        compiler_params=PARAMS,
        cost_estimate=SMALL,
        name="cycle_sums",
    )(base, ints, labels, own_labels, *rights)


def owner_kernel(occ_local, *refs):
    *values, out_ref = refs
    count, rows, _ = out_ref.shape
    virt = rows // occ_local
    for half in range(2):
        keep, near, far = values[half * 3 : half * 3 + 3]
        total = keep[0] + near[0] + far[0]
        for a in range(virt // 2):
            for target in range(count):
                begin = (a * count + target) * occ_local
                at = (half * virt // 2 + a) * occ_local
                out_ref[target, at : at + occ_local, :] = total[begin : begin + occ_local, :]


def owner_blocks(low, high, count, occ_local):
    _, height, width = low[0].shape
    rows = 2 * height // count
    return pl.pallas_call(
        functools.partial(owner_kernel, occ_local),
        grid=(1,),
        in_specs=[pl.BlockSpec((1, height, width), lambda step: (0, 0, 0))] * 6,
        out_specs=pl.BlockSpec((count, rows, width), lambda step: (0, 0, 0)),
        out_shape=jax.ShapeDtypeStruct((count, rows, width), jnp.float32),
        compiler_params=PARAMS,
        cost_estimate=SMALL,
        name="owner_blocks",
    )(*low, *high)


def update_kernel(occ, occ_local, at, back_ref, ladder_ref, rows_ref, cols_ref, out_ref, cells, rows):
    sources, height, width = back_ref.shape
    count = width // occ
    pad = -(-occ_local // 8) * 8
    for a in range(height // occ_local):
        for source in range(sources):
            value = back_ref[source, a * occ_local : (a + 1) * occ_local, :]
            for b in range(count):
                at = ((a * sources + source) * count + b) * pad
                cells[at : at + occ_local, 0:occ] = value[:, b * occ : (b + 1) * occ]
    for i in range(occ_local):
        value = cells[pl.ds(i, rows.shape[0], stride=pad), :]
        rows[:, i * occ : (i + 1) * occ] = value[:, 0:occ]
    out_ref[...] = (ladder_ref[...] + rows[...]) / (rows_ref[...] - cols_ref[...])


def with_cycle(part, back, ladder, row_energy, col_energy, occ, occ_local):
    sources, rows, width = back.shape
    columns = ladder.shape[1]
    height = rows // occ_local * sources * width // occ
    pad = -(-occ_local // 8) * 8
    block = pl.BlockSpec((height, columns), lambda step, at: (at[0], 0))
    return pl.pallas_call(
        functools.partial(update_kernel, occ, occ_local),
        grid_spec=pltpu.PrefetchScalarGridSpec(
            num_scalar_prefetch=1,
            grid=(1,),
            in_specs=[
                pl.BlockSpec(back.shape, lambda step, at: (0, 0, 0)),
                block,
                pl.BlockSpec((height, 1), lambda step, at: (at[0], 0)),
                pl.BlockSpec((1, columns), lambda step, at: (0, 0)),
            ],
            out_specs=block,
            scratch_shapes=[
                pltpu.VMEM((height * pad, 128), jnp.float32),
                pltpu.VMEM((height, columns), jnp.float32),
            ],
        ),
        out_shape=jax.ShapeDtypeStruct(ladder.shape, jnp.float32),
        input_output_aliases={2: 0},
        compiler_params=PARAMS,
        cost_estimate=SMALL,
        name="with_cycle",
    )(
        jnp.full((1,), part, jnp.int32),
        back,
        ladder,
        row_energy,
        col_energy,
    )


def ladder_kernel(fresh, start, packed_ref, rank_ref, label_ref, own_ref, amps_ref, *refs):
    total_ref, (out_ref, high_ref, low_ref) = (None, refs) if fresh else (refs[0], refs[1:])

    @pl.when(pl.program_id(0) == 0)
    def _():
        high, low = halves(amps_ref[...])
        high_ref[...] = high
        low_ref[...] = low

    size, tile, window = packed_ref.shape
    wide = rank_ref.shape[2]
    total = None if fresh else total_ref[...]
    for n in range(size):
        pick = lax.broadcasted_iota(jnp.int32, (window, wide), 0) == rank_ref[n]
        pick = pick.astype(jnp.float32).astype(jnp.bfloat16)
        high, low = halves(packed_ref[n])
        ints = dot(high, pick) + dot(low, pick)
        ints = jnp.where(own_ref[...] == label_ref[n], ints, jnp.float32(0.0))
        high, low = halves(ints)
        at = slice(n * wide, (n + 1) * wide)
        term = dot(low, high_ref[at, :]) + dot(high, low_ref[at, :]) + dot(high, high_ref[at, :])
        total = term if total is None else total + term
    out_ref[...] = total


def ladder_term(start, packed, ranks, labels, own_pairs, amps, total=None):
    blocks, rows, window = packed.shape
    wide = ranks.shape[2]
    depth, columns = amps.shape
    size = depth // wide
    fresh = total is None
    out_block = pl.BlockSpec((TILE, columns), lambda m, start: (m, 0))
    small = pl.BlockSpec((size, 1, wide), lambda m, start: (start[0], 0, 0))
    return pl.pallas_call(
        functools.partial(ladder_kernel, fresh),
        grid_spec=pltpu.PrefetchScalarGridSpec(
            num_scalar_prefetch=1,
            grid=(rows // TILE,),
            in_specs=[
                pl.BlockSpec((size, TILE, window), lambda m, start: (start[0], m, 0)),
                small,
                small,
                pl.BlockSpec((TILE, 1), lambda m, start: (m, 0)),
                pl.BlockSpec((depth, columns), lambda m, start: (0, 0)),
            ]
            + ([] if fresh else [out_block]),
            out_specs=out_block,
            scratch_shapes=[pltpu.VMEM((depth, columns), jnp.bfloat16)] * 2,
        ),
        out_shape=jax.ShapeDtypeStruct((rows, columns), jnp.float32),
        input_output_aliases={} if fresh else {6: 0},
        compiler_params=PARAMS,
        cost_estimate=SMALL,
        name="ladder_term",
    )(
        jnp.reshape(start // size, (1,)).astype(jnp.int32),
        packed,
        ranks,
        labels,
        own_pairs,
        amps,
        *([] if fresh else [total]),
    )


def body(amps, ladder_ints, cycle_ints, virt_irrep, occ_irrep, virt_energy, occ_energy):
    row_count = lax.axis_size("row")
    col_count = lax.axis_size("col")
    row_index = lax.axis_index("row")
    col_index = lax.axis_index("col")
    virt_total = virt_irrep.shape[0]
    occ_total = occ_irrep.shape[0]
    virt_local = virt_total // row_count
    occ_local = occ_total // col_count
    virt_cols = virt_total // col_count
    pair_rows, columns = amps.shape
    ladder_cols = ladder_ints.shape[1]
    virt_pairs = pair_labels(virt_irrep, virt_irrep)
    own_pairs = lax.dynamic_slice_in_dim(virt_pairs, row_index * pair_rows, pair_rows)
    mixed_pairs = pair_labels(virt_irrep, occ_irrep)
    cycle_rows = virt_local * occ_total
    own_mixed = lax.dynamic_slice_in_dim(mixed_pairs, row_index * cycle_rows, cycle_rows)
    barrier = lax.optimization_barrier

    def swap(value, flip):
        return lax.ppermute(value, "row", [(i, i ^ flip) for i in range(row_count)])

    half_virt = virt_local // 2
    half_rows = pair_rows // 2
    first, second = amps[:half_rows], amps[half_rows:]

    def to_cycle(value):
        blocks = value.reshape(half_virt, col_count, virt_cols, columns).transpose(1, 0, 2, 3)
        return lax.all_to_all(blocks, "col", split_axis=0, concat_axis=0, tiled=True)

    first_2, second_1 = swap(first, 2), swap(second, 1)
    moved = to_cycle(first)

    blocks = virt_pairs.reshape(col_count, ladder_cols)
    place = jnp.arange(ladder_cols)
    same = (blocks[:, :, None] == blocks[:, None, :]) & (place[None, None, :] < place[None, :, None])
    rank = jnp.sum(same, axis=2, dtype=jnp.int32)
    turns = jnp.max(rank) // WINDOW + 1

    own_virt = lax.dynamic_slice_in_dim(virt_energy, row_index * virt_local, virt_local)
    own_occ = lax.dynamic_slice_in_dim(occ_energy, col_index * occ_local, occ_local)
    row_energy = (own_virt[:, None] + virt_energy[None, :]).reshape(-1)[:, None]
    col_energy = (own_occ[:, None] + occ_energy[None, :]).reshape(-1)[None, :]

    mixed_rows, mixed_cols = mixed_pairs[:, None], own_mixed[None, :]
    small = (mixed_rows, mixed_cols, row_energy, col_energy, rank, turns)
    held_first, held, first_2, second_1, moved, small = barrier(
        (first, second, first_2, second_1, moved, small)
    )
    mixed_rows, mixed_cols, row_energy, col_energy, rank, turns = small
    first_1, second_2 = swap(held_first, 1), swap(held, 2)
    rights = to_cycle_rows(moved, occ_total)
    moved = to_cycle(held)
    moved, first_1, second_2, first_2, second_1 = barrier(
        (moved, first_1, second_2, first_2, second_1)
    )
    first_3, second_3 = swap(first_2, 1), swap(second_1, 2)
    rights = rights + to_cycle_rows(moved, occ_total)

    own_rank = lax.dynamic_index_in_dim(rank, col_index, 0, keepdims=False)
    own_block = lax.dynamic_index_in_dim(blocks, col_index, 0, keepdims=False)
    masked_ints = jnp.where(own_pairs[:, None] == own_block[None, :], ladder_ints, jnp.float32(0.0))

    def packed_ints(turn):
        pick = own_rank[:, None] == turn * WINDOW + jnp.arange(WINDOW)[None, :]
        return jnp.dot(
            masked_ints,
            pick.astype(jnp.float32),
            precision=lax.Precision.HIGH,
            preferred_element_type=jnp.float32,
        )

    def gathered(packed):
        return lax.all_gather(packed, "col", axis=0, tiled=False)

    def ladder_from(packed, turn, pieces, total=None):
        for flip, half, value in pieces:
            start = (row_index ^ flip) * (pair_rows // ladder_cols)
            start += half * (half_rows // ladder_cols)
            total = ladder_term(
                start,
                packed,
                rank[:, None, :] - turn * WINDOW,
                blocks[:, None, :],
                own_pairs[:, None],
                value,
                total,
            )
        return total

    packed, rights = barrier((packed_ints(0), rights))
    packed = gathered(packed)

    sums = functools.partial(
        cycle_sums, row_index=row_index, ints=cycle_ints, labels=mixed_rows,
        own_labels=mixed_cols,
    )
    def pass_on(keep, near):
        return swap(keep[0][1:] + near[0][1:], 1), swap(keep[1][1:] + near[1][1:], 2)

    def send(values):
        return swap(values[0], 2), swap(values[1], 1)

    def owned(keep, near, far):
        return owner_blocks(
            (keep[0], near[0], far[0]), (keep[1], near[1], far[1]), col_count, occ_local
        )

    def to_owner(blocks):
        return lax.all_to_all(blocks, "col", split_axis=0, concat_axis=0, tiled=True)

    def part_sums(part, rights):
        values = sums(part, rights=rights)
        return values[:2], values[2:]

    pieces = [(0, 0, first), (0, 1, second), (2, 0, first_2), (1, 1, second_1)]
    pieces += [(1, 0, first_1), (2, 1, second_2)]
    out_0, keep_0 = part_sums(0, rights)
    near_0 = send(out_0)
    rights, keep_0 = barrier((rights, keep_0))
    out_1, keep_1 = part_sums(1, rights)
    rights, keep_1 = barrier((rights, keep_1))
    out_2, keep_2 = part_sums(2, rights)
    packed, keep_2 = barrier((packed, keep_2))
    ladder = ladder_from(packed, 0, pieces[:1])

    rights, ladder, first_3, second_3, near_0, keep_0, out_1, keep_1, out_2, keep_2 = barrier(
        (rights, ladder, first_3, second_3, near_0, keep_0, out_1, keep_1, out_2, keep_2)
    )
    pieces += [(3, 0, first_3), (3, 1, second_3)]
    far_0, near_1 = pass_on(keep_0, near_0), send(out_1)
    ladder = ladder_from(packed, 0, pieces[1:3], ladder)
    ladder, far_0 = barrier((ladder, far_0))
    blocks_0 = owned(keep_0, near_0, far_0)

    rights, ladder, _, near_1, keep_1, out_2, keep_2 = barrier(
        (rights, ladder, blocks_0, near_1, keep_1, out_2, keep_2)
    )
    far_1, near_2 = pass_on(keep_1, near_1), send(out_2)
    out_3, keep_3 = part_sums(3, rights)
    keep_3, far_1 = barrier((keep_3, far_1))
    blocks_1 = owned(keep_1, near_1, far_1)
    _, ladder = barrier((blocks_1, ladder))
    ladder = ladder_from(packed, 0, pieces[3:4], ladder)

    ladder, near_2, keep_2, out_3, keep_3 = barrier((ladder, near_2, keep_2, out_3, keep_3))
    far_2, near_3 = pass_on(keep_2, near_2), send(out_3)
    ladder = ladder_from(packed, 0, pieces[4:6], ladder)
    ladder, far_2 = barrier((ladder, far_2))
    blocks_2 = owned(keep_2, near_2, far_2)

    ladder, _, near_3, keep_3 = barrier((ladder, blocks_2, near_3, keep_3))
    far_3 = pass_on(keep_3, near_3)
    ladder = ladder_from(packed, 0, pieces[6:7], ladder)
    ladder, far_3 = barrier((ladder, far_3))
    blocks_3 = owned(keep_3, near_3, far_3)
    back_0, back_1, back_2, back_3 = map(to_owner, (blocks_0, blocks_1, blocks_2, blocks_3))
    _, ladder = barrier((blocks_3, ladder))
    ladder = ladder_from(packed, 0, pieces[7:], ladder)
    backs = [back_0, back_1, back_2, back_3]
    update = ladder
    for part in range(PARTS):
        update = with_cycle(
            part, backs[part], update, row_energy, col_energy, occ_total, occ_local
        )
    return lax.fori_loop(
        1,
        turns,
        lambda turn, total: total
        + ladder_from(gathered(packed_ints(turn)), turn, pieces) / (row_energy - col_energy),
        update,
    )


def plain_body(
    amps, ladder_ints, cycle_ints, virt_irrep, occ_irrep, virt_energy, occ_energy
):
    high = lax.Precision.HIGH
    row_count = lax.axis_size("row")
    col_count = lax.axis_size("col")
    row_index = lax.axis_index("row")
    col_index = lax.axis_index("col")
    virt_total = virt_irrep.shape[0]
    occ_total = occ_irrep.shape[0]
    virt_local = virt_total // row_count
    occ_local = occ_total // col_count
    virt_cols = virt_total // col_count
    pair_rows = amps.shape[0]
    virt_pairs = pair_labels(virt_irrep, virt_irrep)
    own_pairs = lax.dynamic_slice_in_dim(virt_pairs, row_index * pair_rows, pair_rows)
    rows_full = lax.all_gather(ladder_ints, "col", axis=1, tiled=True)
    masked = jnp.where(own_pairs[:, None] == virt_pairs[None, :], rows_full, jnp.float32(0.0))
    ladder = jnp.dot(
        masked,
        lax.all_gather(amps, "row", axis=0, tiled=True),
        precision=high,
        preferred_element_type=jnp.float32,
    )
    blocks = amps.reshape(virt_local, virt_total, occ_local, occ_total)
    moved = lax.all_to_all(blocks, "col", split_axis=1, concat_axis=2, tiled=True)
    cycle_amps = moved.transpose(0, 2, 1, 3).reshape(virt_local * occ_total, virt_cols * occ_total)
    mixed_pairs = pair_labels(virt_irrep, occ_irrep)
    cycle_rows = cycle_amps.shape[0]
    own_mixed = lax.dynamic_slice_in_dim(mixed_pairs, row_index * cycle_rows, cycle_rows)
    part = cycle_ints
    part = jnp.where(mixed_pairs[:, None] == own_mixed[None, :], part, jnp.float32(0.0))
    cycle = lax.psum_scatter(
        jnp.dot(part, cycle_amps, precision=high, preferred_element_type=jnp.float32),
        "row",
        scatter_dimension=0,
        tiled=True,
    )
    cycle_blocks = cycle.reshape(virt_local, occ_total, virt_cols, occ_total)
    returned = lax.all_to_all(cycle_blocks, "col", split_axis=1, concat_axis=2, tiled=True)
    cycle_back = returned.transpose(0, 2, 1, 3).reshape(
        virt_local * virt_total, occ_local * occ_total
    )
    own_virt = lax.dynamic_slice_in_dim(virt_energy, row_index * virt_local, virt_local)
    own_occ = lax.dynamic_slice_in_dim(occ_energy, col_index * occ_local, occ_local)
    row_energy = (own_virt[:, None] + virt_energy[None, :]).reshape(-1)
    col_energy = (own_occ[:, None] + occ_energy[None, :]).reshape(-1)
    return (ladder + cycle_back) / (row_energy[:, None] - col_energy[None, :])


def solution(mesh):
    placed = (P("row", "col"), P("row", "col"), P(None, "row"), P(), P(), P(), P())
    plan = body if mesh.shape["row"] == 4 else plain_body
    return jax.shard_map(
        plan, mesh=mesh, in_specs=placed, out_specs=P("row", "col"), check_vma=False
    )
```

```python
import functools

import jax
import jax.numpy as jnp
from jax import lax
from jax.experimental import pallas as pl
from jax.experimental.pallas import tpu as pltpu
from jax.sharding import PartitionSpec as P

PARTS = 4
WINDOW = 128
TILE = 256
SMALL = pl.CostEstimate(flops=0, bytes_accessed=0, transcendentals=0)
PARAMS = pltpu.CompilerParams(vmem_limit_bytes=56 * 1024 * 1024)


def pair_labels(first, second):
    return jnp.bitwise_xor(first[:, None], second[None, :]).reshape(-1)


def halves(value):
    high = value.astype(jnp.bfloat16)
    return high, (value - high.astype(jnp.float32)).astype(jnp.bfloat16)


def dot(left, right):
    return jnp.dot(left, right, preferred_element_type=jnp.float32)


def to_cycle_kernel(occ, moved_ref, high_ref, low_ref, cells, rows):
    sources, _, depth, width = moved_ref.shape
    count = width // occ
    for source in range(sources):
        value = moved_ref[source, 0]
        for k in range(count):
            at = (source * count + k) * 8
            cells[at : at + depth, 0:occ] = value[:, k * occ : (k + 1) * occ]
    for d in range(depth):
        value = cells[pl.ds(d, sources * count, stride=8), :]
        rows[:, d * occ : (d + 1) * occ] = value[:, 0:occ]
    high, low = halves(rows[...])
    high_ref[...] = high
    low_ref[...] = low


def to_cycle_rows(moved, occ):
    sources, count, depth, width = moved.shape
    height = sources * width // occ
    shape = jax.ShapeDtypeStruct((count * height, depth * occ), jnp.bfloat16)
    return pl.pallas_call(
        functools.partial(to_cycle_kernel, occ),
        grid=(count,),
        in_specs=[pl.BlockSpec((sources, 1, depth, width), lambda c: (0, c, 0, 0))],
        out_specs=[pl.BlockSpec((height, depth * occ), lambda c: (c, 0))] * 2,
        out_shape=[shape, shape],
        scratch_shapes=[
            pltpu.VMEM((height * 8 + 8, 128), jnp.float32),
            pltpu.VMEM((height, depth * occ), jnp.float32),
        ],
        compiler_params=PARAMS,
        cost_estimate=SMALL,
        name="to_cycle_rows",
    )(moved)


def cycle_kernel(
    base, ints_ref, rows_ref, own_ref, high_0, low_0, high_1, low_1, send_y, send_x, keep_y, keep_x
):
    step = pl.program_id(0)
    masked = jnp.where(rows_ref[...] == own_ref[...], ints_ref[...], jnp.float32(0.0))
    high, low = halves(masked)
    middle = high_0.shape[0]
    total = dot(low[:, :middle], high_0[...]) + dot(low[:, middle:], high_1[...])
    total += dot(high[:, :middle], low_0[...]) + dot(high[:, middle:], low_1[...])
    total += dot(high[:, :middle], high_0[...]) + dot(high[:, middle:], high_1[...])
    half = total.shape[0] // 2

    @pl.when(step < 2)
    def _():
        send_y[0] = total[:half]

    @pl.when(step >= 2)
    def _():
        keep_y[0] = total[:half]

    @pl.when(step % 2 == 0)
    def _():
        send_x[0] = total[half:]

    @pl.when(step % 2 == 1)
    def _():
        keep_x[0] = total[half:]


def cycle_sums(part, row_index, ints, labels, own_labels, rights):
    depth = ints.shape[1]
    width = rights[0].shape[1]
    height = ints.shape[0] // 4 // PARTS
    base = jnp.reshape(row_index, (1,)).astype(jnp.int32)

    def at(step, base):
        return (base[0] ^ (3 - step)) * PARTS + part, 0

    def still(step, base):
        return 0, 0

    shape = jax.ShapeDtypeStruct((2, height // 2, width), jnp.float32)
    block = (1, height // 2, width)
    return pl.pallas_call(
        cycle_kernel,
        grid_spec=pltpu.PrefetchScalarGridSpec(
            num_scalar_prefetch=1,
            grid=(4,),
            in_specs=[
                pl.BlockSpec((height, depth), at),
                pl.BlockSpec((height, 1), at),
                pl.BlockSpec((1, depth), still),
            ]
            + [pl.BlockSpec(value.shape, still) for value in rights],
            out_specs=[
                pl.BlockSpec(block, lambda step, base: (jnp.where(step == 0, 1, 0), 0, 0)),
                pl.BlockSpec(block, lambda step, base: (jnp.where(step < 2, 1, 0), 0, 0)),
                pl.BlockSpec(block, lambda step, base: (jnp.where(step < 3, 1, 0), 0, 0)),
                pl.BlockSpec(block, lambda step, base: (jnp.where(step < 2, 1, 0), 0, 0)),
            ],
        ),
        out_shape=[shape] * 4,
        compiler_params=PARAMS,
        cost_estimate=SMALL,
        name="cycle_sums",
    )(base, ints, labels, own_labels, *rights)


def owner_kernel(occ_local, *refs):
    *values, out_ref = refs
    count, rows, _ = out_ref.shape
    virt = rows // occ_local
    for half in range(2):
        keep, near, far = values[half * 3 : half * 3 + 3]
        total = keep[0] + near[0] + far[0]
        for a in range(virt // 2):
            for target in range(count):
                begin = (a * count + target) * occ_local
                at = (half * virt // 2 + a) * occ_local
                out_ref[target, at : at + occ_local, :] = total[begin : begin + occ_local, :]


def owner_blocks(low, high, count, occ_local):
    _, height, width = low[0].shape
    rows = 2 * height // count
    return pl.pallas_call(
        functools.partial(owner_kernel, occ_local),
        grid=(1,),
        in_specs=[pl.BlockSpec((1, height, width), lambda step: (0, 0, 0))] * 6,
        out_specs=pl.BlockSpec((count, rows, width), lambda step: (0, 0, 0)),
        out_shape=jax.ShapeDtypeStruct((count, rows, width), jnp.float32),
        compiler_params=PARAMS,
        cost_estimate=SMALL,
        name="owner_blocks",
    )(*low, *high)


def update_kernel(occ, occ_local, at, back_ref, ladder_ref, rows_ref, cols_ref, out_ref, cells, rows):
    sources, height, width = back_ref.shape
    count = width // occ
    pad = -(-occ_local // 8) * 8
    for a in range(height // occ_local):
        for source in range(sources):
            value = back_ref[source, a * occ_local : (a + 1) * occ_local, :]
            for b in range(count):
                at = ((a * sources + source) * count + b) * pad
                cells[at : at + occ_local, 0:occ] = value[:, b * occ : (b + 1) * occ]
    for i in range(occ_local):
        value = cells[pl.ds(i, rows.shape[0], stride=pad), :]
        rows[:, i * occ : (i + 1) * occ] = value[:, 0:occ]
    out_ref[...] = (ladder_ref[...] + rows[...]) / (rows_ref[...] - cols_ref[...])


def with_cycle(part, back, ladder, row_energy, col_energy, occ, occ_local):
    sources, rows, width = back.shape
    columns = ladder.shape[1]
    height = rows // occ_local * sources * width // occ
    pad = -(-occ_local // 8) * 8
    block = pl.BlockSpec((height, columns), lambda step, at: (at[0], 0))
    return pl.pallas_call(
        functools.partial(update_kernel, occ, occ_local),
        grid_spec=pltpu.PrefetchScalarGridSpec(
            num_scalar_prefetch=1,
            grid=(1,),
            in_specs=[
                pl.BlockSpec(back.shape, lambda step, at: (0, 0, 0)),
                block,
                pl.BlockSpec((height, 1), lambda step, at: (at[0], 0)),
                pl.BlockSpec((1, columns), lambda step, at: (0, 0)),
            ],
            out_specs=block,
            scratch_shapes=[
                pltpu.VMEM((height * pad + pad, 128), jnp.float32),
                pltpu.VMEM((height, columns), jnp.float32),
            ],
        ),
        out_shape=jax.ShapeDtypeStruct(ladder.shape, jnp.float32),
        input_output_aliases={2: 0},
        compiler_params=PARAMS,
        cost_estimate=SMALL,
        name="with_cycle",
    )(
        jnp.full((1,), part, jnp.int32),
        back,
        ladder,
        row_energy,
        col_energy,
    )


def ladder_kernel(fresh, start, packed_ref, rank_ref, label_ref, own_ref, amps_ref, *refs):
    total_ref, (out_ref, high_ref, low_ref) = (None, refs) if fresh else (refs[0], refs[1:])

    @pl.when(pl.program_id(0) == 0)
    def _():
        high, low = halves(amps_ref[...])
        high_ref[...] = high
        low_ref[...] = low

    size, tile, window = packed_ref.shape
    wide = rank_ref.shape[2]
    total = None if fresh else total_ref[...]
    for n in range(size):
        pick = lax.broadcasted_iota(jnp.int32, (window, wide), 0) == rank_ref[n]
        pick = pick.astype(jnp.float32).astype(jnp.bfloat16)
        high, low = halves(packed_ref[n])
        ints = dot(high, pick) + dot(low, pick)
        ints = jnp.where(own_ref[...] == label_ref[n], ints, jnp.float32(0.0))
        high, low = halves(ints)
        at = slice(n * wide, (n + 1) * wide)
        term = dot(low, high_ref[at, :]) + dot(high, low_ref[at, :]) + dot(high, high_ref[at, :])
        total = term if total is None else total + term
    out_ref[...] = total


def ladder_term(start, packed, ranks, labels, own_pairs, amps, total=None):
    blocks, rows, window = packed.shape
    wide = ranks.shape[2]
    depth, columns = amps.shape
    size = depth // wide
    fresh = total is None
    out_block = pl.BlockSpec((TILE, columns), lambda m, start: (m, 0))
    small = pl.BlockSpec((size, 1, wide), lambda m, start: (start[0], 0, 0))
    return pl.pallas_call(
        functools.partial(ladder_kernel, fresh),
        grid_spec=pltpu.PrefetchScalarGridSpec(
            num_scalar_prefetch=1,
            grid=(rows // TILE,),
            in_specs=[
                pl.BlockSpec((size, TILE, window), lambda m, start: (start[0], m, 0)),
                small,
                small,
                pl.BlockSpec((TILE, 1), lambda m, start: (m, 0)),
                pl.BlockSpec((depth, columns), lambda m, start: (0, 0)),
            ]
            + ([] if fresh else [out_block]),
            out_specs=out_block,
            scratch_shapes=[pltpu.VMEM((depth, columns), jnp.bfloat16)] * 2,
        ),
        out_shape=jax.ShapeDtypeStruct((rows, columns), jnp.float32),
        input_output_aliases={} if fresh else {6: 0},
        compiler_params=PARAMS,
        cost_estimate=SMALL,
        name="ladder_term",
    )(
        jnp.reshape(start // size, (1,)).astype(jnp.int32),
        packed,
        ranks,
        labels,
        own_pairs,
        amps,
        *([] if fresh else [total]),
    )


def body(amps, ladder_ints, cycle_ints, virt_irrep, occ_irrep, virt_energy, occ_energy):
    row_count = lax.axis_size("row")
    col_count = lax.axis_size("col")
    row_index = lax.axis_index("row")
    col_index = lax.axis_index("col")
    virt_total = virt_irrep.shape[0]
    occ_total = occ_irrep.shape[0]
    virt_local = virt_total // row_count
    occ_local = occ_total // col_count
    virt_cols = virt_total // col_count
    pair_rows, columns = amps.shape
    ladder_cols = ladder_ints.shape[1]
    virt_pairs = pair_labels(virt_irrep, virt_irrep)
    own_pairs = lax.dynamic_slice_in_dim(virt_pairs, row_index * pair_rows, pair_rows)
    mixed_pairs = pair_labels(virt_irrep, occ_irrep)
    cycle_rows = virt_local * occ_total
    own_mixed = lax.dynamic_slice_in_dim(mixed_pairs, row_index * cycle_rows, cycle_rows)
    barrier = lax.optimization_barrier

    def swap(value, flip):
        return lax.ppermute(value, "row", [(i, i ^ flip) for i in range(row_count)])

    half_virt = virt_local // 2
    half_rows = pair_rows // 2
    first, second = amps[:half_rows], amps[half_rows:]

    def to_cycle(value):
        blocks = value.reshape(half_virt, col_count, virt_cols, columns).transpose(1, 0, 2, 3)
        return lax.all_to_all(blocks, "col", split_axis=0, concat_axis=0, tiled=True)

    first_2, second_1 = swap(first, 2), swap(second, 1)
    moved = to_cycle(first)

    blocks = virt_pairs.reshape(col_count, ladder_cols)
    place = jnp.arange(ladder_cols)
    same = (blocks[:, :, None] == blocks[:, None, :]) & (place[None, None, :] < place[None, :, None])
    rank = jnp.sum(same, axis=2, dtype=jnp.int32)
    turns = jnp.max(rank) // WINDOW + 1

    own_virt = lax.dynamic_slice_in_dim(virt_energy, row_index * virt_local, virt_local)
    own_occ = lax.dynamic_slice_in_dim(occ_energy, col_index * occ_local, occ_local)
    row_energy = (own_virt[:, None] + virt_energy[None, :]).reshape(-1)[:, None]
    col_energy = (own_occ[:, None] + occ_energy[None, :]).reshape(-1)[None, :]

    mixed_rows, mixed_cols = mixed_pairs[:, None], own_mixed[None, :]
    small = (mixed_rows, mixed_cols, row_energy, col_energy, rank, turns)
    held_first, held, first_2, second_1, moved, small = barrier(
        (first, second, first_2, second_1, moved, small)
    )
    mixed_rows, mixed_cols, row_energy, col_energy, rank, turns = small
    first_1, second_2 = swap(held_first, 1), swap(held, 2)
    rights = to_cycle_rows(moved, occ_total)
    moved = to_cycle(held)
    moved, first_1, second_2, first_2, second_1 = barrier(
        (moved, first_1, second_2, first_2, second_1)
    )
    first_3, second_3 = swap(first_2, 1), swap(second_1, 2)
    rights = rights + to_cycle_rows(moved, occ_total)

    own_rank = lax.dynamic_index_in_dim(rank, col_index, 0, keepdims=False)
    own_block = lax.dynamic_index_in_dim(blocks, col_index, 0, keepdims=False)
    masked_ints = jnp.where(own_pairs[:, None] == own_block[None, :], ladder_ints, jnp.float32(0.0))

    def packed_ints(turn):
        pick = own_rank[:, None] == turn * WINDOW + jnp.arange(WINDOW)[None, :]
        return jnp.dot(
            masked_ints,
            pick.astype(jnp.float32),
            precision=lax.Precision.HIGH,
            preferred_element_type=jnp.float32,
        )

    def gathered(packed):
        return lax.all_gather(packed, "col", axis=0, tiled=False)

    def ladder_from(packed, turn, pieces, total=None):
        for flip, half, value in pieces:
            start = (row_index ^ flip) * (pair_rows // ladder_cols)
            start += half * (half_rows // ladder_cols)
            total = ladder_term(
                start,
                packed,
                rank[:, None, :] - turn * WINDOW,
                blocks[:, None, :],
                own_pairs[:, None],
                value,
                total,
            )
        return total

    packed, rights = barrier((packed_ints(0), rights))
    packed = gathered(packed)

    sums = functools.partial(
        cycle_sums, row_index=row_index, ints=cycle_ints, labels=mixed_rows,
        own_labels=mixed_cols,
    )
    def pass_on(keep, near):
        return swap(keep[0][1:] + near[0][1:], 1), swap(keep[1][1:] + near[1][1:], 2)

    def send(values):
        return swap(values[0], 2), swap(values[1], 1)

    def owned(keep, near, far):
        return owner_blocks(
            (keep[0], near[0], far[0]), (keep[1], near[1], far[1]), col_count, occ_local
        )

    def to_owner(blocks):
        return lax.all_to_all(blocks, "col", split_axis=0, concat_axis=0, tiled=True)

    def part_sums(part, rights):
        values = sums(part, rights=rights)
        return values[:2], values[2:]

    pieces = [(0, 0, first), (0, 1, second), (2, 0, first_2), (1, 1, second_1)]
    pieces += [(1, 0, first_1), (2, 1, second_2)]
    out_0, keep_0 = part_sums(0, rights)
    near_0 = send(out_0)
    rights, keep_0 = barrier((rights, keep_0))
    out_1, keep_1 = part_sums(1, rights)
    rights, keep_1 = barrier((rights, keep_1))
    out_2, keep_2 = part_sums(2, rights)
    packed, keep_2 = barrier((packed, keep_2))
    ladder = ladder_from(packed, 0, pieces[:1])

    rights, ladder, first_3, second_3, near_0, keep_0, out_1, keep_1, out_2, keep_2 = barrier(
        (rights, ladder, first_3, second_3, near_0, keep_0, out_1, keep_1, out_2, keep_2)
    )
    pieces += [(3, 0, first_3), (3, 1, second_3)]
    far_0, near_1 = pass_on(keep_0, near_0), send(out_1)
    ladder = ladder_from(packed, 0, pieces[1:3], ladder)
    ladder, far_0 = barrier((ladder, far_0))
    blocks_0 = owned(keep_0, near_0, far_0)

    rights, ladder, _, near_1, keep_1, out_2, keep_2 = barrier(
        (rights, ladder, blocks_0, near_1, keep_1, out_2, keep_2)
    )
    far_1, near_2 = pass_on(keep_1, near_1), send(out_2)
    out_3, keep_3 = part_sums(3, rights)
    keep_3, far_1 = barrier((keep_3, far_1))
    blocks_1 = owned(keep_1, near_1, far_1)
    _, ladder = barrier((blocks_1, ladder))
    ladder = ladder_from(packed, 0, pieces[3:4], ladder)

    ladder, near_2, keep_2, out_3, keep_3 = barrier((ladder, near_2, keep_2, out_3, keep_3))
    far_2, near_3 = pass_on(keep_2, near_2), send(out_3)
    ladder = ladder_from(packed, 0, pieces[4:6], ladder)
    ladder, far_2 = barrier((ladder, far_2))
    blocks_2 = owned(keep_2, near_2, far_2)

    ladder, _, near_3, keep_3 = barrier((ladder, blocks_2, near_3, keep_3))
    far_3 = pass_on(keep_3, near_3)
    ladder = ladder_from(packed, 0, pieces[6:7], ladder)
    ladder, far_3 = barrier((ladder, far_3))
    blocks_3 = owned(keep_3, near_3, far_3)
    back_0, back_1, back_2, back_3 = map(to_owner, (blocks_0, blocks_1, blocks_2, blocks_3))
    _, ladder = barrier((blocks_3, ladder))
    ladder = ladder_from(packed, 0, pieces[7:], ladder)
    backs = [back_0, back_1, back_2, back_3]
    update = ladder
    for part in range(PARTS):
        update = with_cycle(
            part, backs[part], update, row_energy, col_energy, occ_total, occ_local
        )
    return lax.fori_loop(
        1,
        turns,
        lambda turn, total: total
        + ladder_from(gathered(packed_ints(turn)), turn, pieces) / (row_energy - col_energy),
        update,
    )


def plain_body(
    amps, ladder_ints, cycle_ints, virt_irrep, occ_irrep, virt_energy, occ_energy
):
    high = lax.Precision.HIGH
    row_count = lax.axis_size("row")
    col_count = lax.axis_size("col")
    row_index = lax.axis_index("row")
    col_index = lax.axis_index("col")
    virt_total = virt_irrep.shape[0]
    occ_total = occ_irrep.shape[0]
    virt_local = virt_total // row_count
    occ_local = occ_total // col_count
    virt_cols = virt_total // col_count
    pair_rows = amps.shape[0]
    virt_pairs = pair_labels(virt_irrep, virt_irrep)
    own_pairs = lax.dynamic_slice_in_dim(virt_pairs, row_index * pair_rows, pair_rows)
    rows_full = lax.all_gather(ladder_ints, "col", axis=1, tiled=True)
    masked = jnp.where(own_pairs[:, None] == virt_pairs[None, :], rows_full, jnp.float32(0.0))
    ladder = jnp.dot(
        masked,
        lax.all_gather(amps, "row", axis=0, tiled=True),
        precision=high,
        preferred_element_type=jnp.float32,
    )
    blocks = amps.reshape(virt_local, virt_total, occ_local, occ_total)
    moved = lax.all_to_all(blocks, "col", split_axis=1, concat_axis=2, tiled=True)
    cycle_amps = moved.transpose(0, 2, 1, 3).reshape(virt_local * occ_total, virt_cols * occ_total)
    mixed_pairs = pair_labels(virt_irrep, occ_irrep)
    cycle_rows = cycle_amps.shape[0]
    own_mixed = lax.dynamic_slice_in_dim(mixed_pairs, row_index * cycle_rows, cycle_rows)
    part = cycle_ints
    part = jnp.where(mixed_pairs[:, None] == own_mixed[None, :], part, jnp.float32(0.0))
    cycle = lax.psum_scatter(
        jnp.dot(part, cycle_amps, precision=high, preferred_element_type=jnp.float32),
        "row",
        scatter_dimension=0,
        tiled=True,
    )
    cycle_blocks = cycle.reshape(virt_local, occ_total, virt_cols, occ_total)
    returned = lax.all_to_all(cycle_blocks, "col", split_axis=1, concat_axis=2, tiled=True)
    cycle_back = returned.transpose(0, 2, 1, 3).reshape(
        virt_local * virt_total, occ_local * occ_total
    )
    own_virt = lax.dynamic_slice_in_dim(virt_energy, row_index * virt_local, virt_local)
    own_occ = lax.dynamic_slice_in_dim(occ_energy, col_index * occ_local, occ_local)
    row_energy = (own_virt[:, None] + virt_energy[None, :]).reshape(-1)
    col_energy = (own_occ[:, None] + occ_energy[None, :]).reshape(-1)
    return (ladder + cycle_back) / (row_energy[:, None] - col_energy[None, :])


def solution(mesh):
    placed = (P("row", "col"), P("row", "col"), P(None, "row"), P(), P(), P(), P())
    plan = body if mesh.shape["row"] == 4 else plain_body
    return jax.shard_map(
        plan, mesh=mesh, in_specs=placed, out_specs=P("row", "col"), check_vma=False
    )
```
